32 devices in a mesh: row: 8 (over y, x, core), col: 4 (over z).
Axes of the slice: x: 2, y: 2, z: 4, core: 2. Of those that a mesh axis runs over, the one named last changes fastest.
Arguments:
- edge_tensor: float32 [1024, 16, 1024], P('row'), may hold values from -0.0234375 to 0.0234375
- site_tensor: float32 [16, 16, 16, 16], replicated, may hold values from -0.375 to 0.375
- left_isometry: float32 [1024, 16, 1024], P('row'), may hold values from -0.0234375 to 0.0234375
- right_isometry: float32 [512, 16, 1024], P('col', None, 'row'), may hold values from -0.03125 to 0.03125
- cotangent: float32 [512, 16, 1024], P('col', None, 'row'), may hold values from -96 to 96
Outputs:
- edge_gradient: float32 [1024, 16, 1024], P('row', 'col')
- site_gradient: float32 [16, 16, 16, 16], replicated
- left_gradient: float32 [1024, 16, 1024], P('row', 'col')
- right_gradient: float32 [512, 16, 1024], P('col', 'row')
The draws below stay inside these ranges and needn't reach their ends.
All inputs are finite; a program needn't handle non-finite values.
Results may differ from the reference program's by a relative error of at most 0.0003.
Values sent between devices are 32-bit elements; how exact they have to be, the bound alone decides.
A program may use at most 192 MiB of HBM per device.

```python
import jax
import jax.numpy as jnp
from jax import lax

CHI = 1024
D2 = 16
COLS = 512
N_ROW = 8


def level_of(key, extent, cuts, least, top_value):
    def one(position, shards_of):
        draws = jax.random.uniform(jax.random.fold_in(jax.random.fold_in(key, 6), position), (shards_of,), jnp.float32, least / len(cuts), top_value / len(cuts))
        return jnp.repeat(jnp.exp(draws), extent[position] // shards_of).reshape((-1,) + (1,) * (len(extent) - position - 1))

    factor_of = one(*cuts[0])
    for cut in cuts[1:]:
        factor_of = factor_of * one(*cut)
    return factor_of


def noise(rng, extent, scale, bound, cuts=(), kind=jnp.bfloat16):
    result = jax.random.normal(rng, extent, jnp.float32) * scale
    if len(cuts) > 0:
        result = level_of(rng, extent, cuts, -0.22, 0.18) * result
    return jnp.clip(result, min=-bound, max=bound).astype(kind)


def setup_inputs(seed: int = 0) -> dict:
    splits = jax.random.split(jax.random.key(seed), 6)
    edge_tensor = noise(splits[0], (CHI, D2, CHI), (4 * CHI * D2) ** -0.5, 0.0234375, ((0, 8),), jnp.float32)
    site_tensor = noise(splits[1], (D2, D2, D2, D2), (D2 * D2) ** -0.5, 0.375, (), jnp.float32)
    left_isometry = noise(splits[2], (CHI, D2, CHI), (4 * CHI * D2) ** -0.5, 0.0234375, ((0, 8),), jnp.float32)
    right_isometry = noise(splits[3], (COLS, D2, CHI), (2 * CHI * D2) ** -0.5, 0.03125, ((0, 4), (2, 8)), jnp.float32)
    cotangent = noise(splits[4], (COLS, D2, CHI), 16.0, 96.0, ((0, 4), (2, 8)), jnp.float32)
    return {"edge_tensor": edge_tensor, "site_tensor": site_tensor, "left_isometry": left_isometry, "right_isometry": right_isometry, "cotangent": cotangent}


def reference(edge_tensor, site_tensor, left_isometry, right_isometry, cotangent):
    highest = lax.Precision.HIGHEST
    square = D2 * D2
    block_rows = CHI // N_ROW
    site_matrix = jnp.transpose(site_tensor, (1, 2, 0, 3)).reshape(square, square)

    def one_block(running, block_index):
        right_acc, site_acc = running
        offset = (block_index * block_rows).astype(jnp.int32)
        edge_rows = lax.dynamic_slice_in_dim(edge_tensor, offset, block_rows, 0)
        left_rows = lax.dynamic_slice_in_dim(left_isometry, offset, block_rows, 0)
        first_section = jnp.einsum('aeb,cfb->acef', edge_rows, right_isometry, precision=highest)
        first_flat = first_section.reshape(block_rows, COLS, square)
        second_flat = jnp.dot(first_flat, site_matrix, precision=highest)
        second_section = second_flat.reshape(block_rows, COLS, D2, D2)
        back_second = jnp.einsum('adk,cgk->acdg', left_rows, cotangent, precision=highest)
        left_part = jnp.einsum('acdg,cgk->adk', second_section, cotangent, precision=highest)
        back_flat = back_second.reshape(block_rows, COLS, square)
        back_first = jnp.dot(back_flat, site_matrix.T, precision=highest).reshape(block_rows, COLS, D2, D2)
        site_acc = site_acc + jnp.dot(first_flat.reshape(-1, square).T, back_flat.reshape(-1, square), precision=highest)
        edge_part = jnp.einsum('acef,cfb->aeb', back_first, right_isometry, precision=highest)
        right_acc = right_acc + jnp.einsum('aeb,acef->cfb', edge_rows, back_first, precision=highest)
        return (right_acc, site_acc), (edge_part, left_part)

    initial = (jnp.zeros((COLS, D2, CHI), jnp.float32), jnp.zeros((square, square), jnp.float32))
    (right_gradient, site_acc), (edge_parts, left_parts) = lax.scan(one_block, initial, jnp.arange(N_ROW, dtype=jnp.int32))
    edge_gradient = edge_parts.reshape(CHI, D2, CHI)
    left_gradient = left_parts.reshape(CHI, D2, CHI)
    site_gradient = jnp.transpose(site_acc.reshape(D2, D2, D2, D2), (2, 0, 1, 3))
    return edge_gradient, site_gradient, left_gradient, right_gradient
```

```python
import functools

import jax
import jax.numpy as jnp
from jax import lax
from jax.experimental import pallas as pl
from jax.experimental.pallas import tpu as pltpu
from jax.sharding import PartitionSpec as P

F32 = jnp.float32
BF16 = jnp.bfloat16
HIGH = lax.Precision.HIGH
NN = (((1,), (0,)), ((), ()))
NT = (((1,), (1,)), ((), ()))
TN = (((0,), (0,)), ((), ()))
BLOCK = 256
TILE = 512


def halves(x):
    hi = x.astype(BF16)
    return hi, (x - hi.astype(F32)).astype(BF16)


def split(x):
    hi = lax.reduce_precision(x, 8, 7)
    return hi.astype(BF16), (x - hi).astype(BF16)


def dot3(xh, xl, yh, yl, dims):
    def dot(x, y):
        return lax.dot_general(x, y, dims, preferred_element_type=F32)

    return dot(xh, yh) + dot(xh, yl) + dot(xl, yh)


def project(xh, xl, wh_ref, wl_ref, oh_ref, ol_ref):
    n = wh_ref.shape[0]
    tile = min(TILE, n)

    def step(i, carry):
        cols = pl.ds(pl.multiple_of(i * tile, tile), tile)
        hi, lo = halves(dot3(xh, xl, wh_ref[cols, :], wl_ref[cols, :], NT))
        oh_ref[:, cols] = hi
        ol_ref[:, cols] = lo
        return carry

    lax.fori_loop(0, n // tile, step, 0)


def gather_pair(ref, start, d, s):
    parts = []
    for k in range(2):
        rows = ref[pl.ds(pl.multiple_of(start + k * d, d), d), :]
        parts.append(jnp.concatenate([rows[:, j * s : (j + 1) * s] for j in range(d)], axis=0))
    return jnp.concatenate(parts, axis=1)


def spread_pair(ref, value, start, d, s):
    for k in range(2):
        rows = [value[j * d : (j + 1) * d, k * s : (k + 1) * s] for j in range(d)]
        ref[pl.ds(pl.multiple_of(start + k * d, d), d), :] = jnp.concatenate(rows, axis=1)


def combine(xh_ref, xl_ref, wh_ref, wl_ref, o_ref):
    n = wh_ref.shape[1]
    tile = min(TILE // 2, n)

    def step(i, carry):
        cols = pl.ds(pl.multiple_of(i * tile, tile), tile)
        o_ref[:, cols] = dot3(xh_ref[...], xl_ref[...], wh_ref[:, cols], wl_ref[:, cols], NN)
        return carry

    lax.fori_loop(0, n // tile, step, 0)


def forward_kernel(d, s, e_ref, sh_ref, sl_ref, rh_ref, rl_ref, ch_ref, cl_ref, left_ref, fh_ref, fl_ref, gh, gl):
    eh, el = halves(e_ref[...])
    project(eh, el, rh_ref, rl_ref, fh_ref, fl_ref)

    def step(i, carry):
        start = i * 2 * d
        x = gather_pair(fh_ref, start, d, s), gather_pair(fl_ref, start, d, s)
        hi, lo = halves(dot3(sh_ref[...], sl_ref[...], *x, NN))
        spread_pair(gh, hi, start, d, s)
        spread_pair(gl, lo, start, d, s)
        return carry

    lax.fori_loop(0, e_ref.shape[0] // (2 * d), step, 0)
    combine(gh, gl, ch_ref, cl_ref, left_ref)


def backward_kernel(
    d, s, e_ref, l_ref, fh_ref, fl_ref, sh_ref, sl_ref, rh_ref, rl_ref, ch_ref, cl_ref,
    edge_ref, right_ref, site_ref, bh, bl, gh, gl,
):
    @pl.when(pl.program_id(0) == 0)
    def _():
        right_ref[...] = jnp.zeros_like(right_ref)
        site_ref[...] = jnp.zeros_like(site_ref)

    lh, ll = halves(l_ref[...])
    project(lh, ll, ch_ref, cl_ref, bh, bl)

    def step(i, carry):
        start = i * 2 * d
        x = gather_pair(bh, start, d, s), gather_pair(bl, start, d, s)
        y = gather_pair(fh_ref, start, d, s), gather_pair(fl_ref, start, d, s)
        hi, lo = halves(dot3(sh_ref[...], sl_ref[...], *x, NN))
        spread_pair(gh, hi, start, d, s)
        spread_pair(gl, lo, start, d, s)
        site_ref[...] += dot3(*x, *y, NT)
        return carry

    lax.fori_loop(0, e_ref.shape[0] // (2 * d), step, 0)
    combine(gh, gl, rh_ref, rl_ref, edge_ref)
    eh, el = halves(e_ref[...])
    tile = min(BLOCK, gh.shape[1])

    def add(i, carry):
        cols = pl.ds(pl.multiple_of(i * tile, tile), tile)
        right_ref[cols, :] += dot3(gh[:, cols], gl[:, cols], eh, el, TN)
        return carry

    lax.fori_loop(0, gh.shape[1] // tile, add, 0)


def whole(shape):
    return pl.BlockSpec(shape, lambda i: (0, 0), pipeline_mode=pl.Buffered(1))


def rows_of(width):
    return pl.BlockSpec((BLOCK, width), lambda i: (i, 0))


PARAMS = pltpu.CompilerParams(dimension_semantics=("arbitrary",), vmem_limit_bytes=58 * 2**20)


def forward(edge, site, right, cot, d, s):
    rows, chi = edge.shape
    wide = d * s
    return pl.pallas_call(
        functools.partial(forward_kernel, d, s),
        grid=(rows // BLOCK,),
        out_shape=[
            jax.ShapeDtypeStruct((rows, chi), F32),
            jax.ShapeDtypeStruct((rows, wide), BF16),
            jax.ShapeDtypeStruct((rows, wide), BF16),
        ],
        in_specs=[rows_of(chi)] + [whole((d * d, d * d))] * 2 + [whole((wide, chi))] * 4,
        out_specs=[rows_of(chi), rows_of(wide), rows_of(wide)],
        scratch_shapes=[pltpu.VMEM((BLOCK, wide), BF16)] * 2,
        compiler_params=PARAMS,
        cost_estimate=pl.CostEstimate(
            flops=12 * rows * wide * chi, bytes_accessed=8 * (rows + wide) * chi, transcendentals=0
        ),
        name="forward",
    )(edge, *site, *right, *cot)


def backward(edge, left, first, site, right, cot, d, s):
    rows, chi = edge.shape
    wide = d * s
    return pl.pallas_call(
        functools.partial(backward_kernel, d, s),
        grid=(rows // BLOCK,),
        out_shape=[
            jax.ShapeDtypeStruct((rows, chi), F32),
            jax.ShapeDtypeStruct((wide, chi), F32),
            jax.ShapeDtypeStruct((d * d, d * d), F32),
        ],
        in_specs=[rows_of(chi)] * 2 + [rows_of(wide)] * 2 + [whole((d * d, d * d))] * 2 + [whole((wide, chi))] * 4,
        out_specs=[rows_of(chi), whole((wide, chi)), whole((d * d, d * d))],
        scratch_shapes=[pltpu.VMEM((BLOCK, wide), BF16)] * 4,
        compiler_params=PARAMS,
        cost_estimate=pl.CostEstimate(
            flops=20 * rows * wide * chi, bytes_accessed=8 * (rows + wide) * chi, transcendentals=0
        ),
        name="backward",
    )(edge, left, *first, *site, *right, *cot)


def swap(x, axis, bit):
    n = lax.axis_size(axis)
    return lax.ppermute(x, axis, [(i, i ^ bit) for i in range(n)])


def gather_row(x):
    s, f, k = x.shape
    n = lax.axis_size("row")
    x = jnp.transpose(x, (1, 0, 2)).reshape(f * s, k)
    groups = [list(range(c, n, 2)) for c in range(2)]
    mine = lax.all_gather(x, "row", axis=0, axis_index_groups=groups)
    other = swap(mine, "row", 1)
    first_core = lax.rem(lax.axis_index("row"), 2) == 0
    even = jnp.where(first_core, mine, other)
    odd = jnp.where(first_core, other, mine)
    return jnp.transpose(jnp.stack([even, odd], 1), (2, 0, 1, 3)).reshape(f * s, n * k)


def sum_to_row(x):
    n = lax.axis_size("row")
    me = lax.axis_index("row")
    x = x.reshape((n, -1) + x.shape[1:])
    bit = 1
    while bit < n:
        x = x.reshape((x.shape[0] // 2, 2) + x.shape[1:])
        mine = lax.rem(me // bit, 2)
        keep = lax.dynamic_index_in_dim(x, mine, 1, keepdims=False)
        send = lax.dynamic_index_in_dim(x, 1 - mine, 1, keepdims=False)
        x = keep + swap(send, "row", bit)
        bit *= 2
    return x[0]


def sum_all(x):
    for axis in ("row", "col"):
        bit = 1
        while bit < lax.axis_size(axis):
            x = x + swap(x, axis, bit)
            bit *= 2
    return x


def with_kernels(edge_tensor, site_tensor, left_isometry, right_isometry, cotangent, n_front=4, n_back=2):
    a, d, chi = edge_tensor.shape
    s = right_isometry.shape[0]
    right = split(gather_row(right_isometry))
    cot = split(gather_row(cotangent))
    site_front = split(jnp.transpose(site_tensor, (3, 0, 2, 1)).reshape(d * d, d * d))
    site_back = split(jnp.transpose(site_tensor, (2, 1, 3, 0)).reshape(d * d, d * d))
    edge = edge_tensor.reshape(a * d, chi)
    left = left_isometry.reshape(a * d, chi)

    def scatter(terms):
        return lax.psum_scatter(terms.reshape(-1, d, chi), "col", scatter_dimension=1, tiled=True)

    n_front = min(n_front, a * d // BLOCK)
    n_back = min(n_back, n_front)
    lefts, firsts = [], []
    for x in jnp.split(edge, n_front):
        terms, fh, fl = forward(x, site_front, right, cot, d, s)
        lefts.append(scatter(terms))
        firsts.append((fh, fl))
    join = n_front // n_back
    edges, rights, sites = [], [], []
    for i, (x, y) in enumerate(zip(jnp.split(edge, n_back), jnp.split(left, n_back))):
        part = firsts[i * join : (i + 1) * join]
        first = tuple(jnp.concatenate([p[k] for p in part], 0) for k in range(2))
        edge_terms, right_terms, site_terms = backward(x, y, first, site_back, right, cot, d, s)
        edges.append(scatter(edge_terms))
        rights.append(right_terms)
        sites.append(site_terms)
    right_sum = sum_to_row(sum(rights))
    right_gradient = jnp.transpose(right_sum.reshape(-1, s, chi), (1, 0, 2))
    site_gradient = jnp.transpose(sum_all(sum(sites)).reshape(d, d, d, d), (1, 3, 2, 0))
    return jnp.concatenate(edges, 0), site_gradient, jnp.concatenate(lefts, 0), right_gradient


def ein(spec, x, y):
    return jnp.einsum(spec, x, y, precision=HIGH)


def without_kernels(edge_tensor, site_tensor, left_isometry, right_isometry, cotangent):
    edge = jnp.transpose(edge_tensor, (1, 0, 2))
    left = jnp.transpose(left_isometry, (1, 0, 2))
    right = lax.all_gather(jnp.transpose(right_isometry, (1, 0, 2)), "row", axis=2, tiled=True)
    cot = lax.all_gather(jnp.transpose(cotangent, (1, 0, 2)), "row", axis=2, tiled=True)
    first = ein("eab,fsb->efas", edge, right)
    second = ein("defg,efas->dgas", site_tensor, first)
    left_terms = ein("dgas,gsc->dac", second, cot)
    left_gradient = lax.psum_scatter(left_terms, "col", scatter_dimension=0, tiled=True)
    back_second = ein("dac,gsc->dgas", left, cot)
    back_first = ein("defg,dgas->efas", site_tensor, back_second)
    edge_terms = ein("efas,fsb->eab", back_first, right)
    edge_gradient = lax.psum_scatter(edge_terms, "col", scatter_dimension=0, tiled=True)
    right_terms = ein("efas,eab->sfb", back_first, edge)
    right_gradient = lax.psum_scatter(right_terms, "row", scatter_dimension=1, tiled=True)
    site_terms = ein("efas,dgas->efdg", first, back_second)
    site_gradient = jnp.transpose(lax.psum(site_terms, ("row", "col")), (2, 0, 1, 3))
    return (
        jnp.transpose(edge_gradient, (1, 0, 2)),
        site_gradient,
        jnp.transpose(left_gradient, (1, 0, 2)),
        right_gradient,
    )


def on_device(*args):
    a, d, chi = args[0].shape
    s = args[3].shape[0]
    n_row, n_col = lax.axis_size("row"), lax.axis_size("col")
    fits = s % 128 == 0 and chi % 256 == 0 and (a * d) % BLOCK == 0 and d % 16 == 0 and n_row > 1
    fits = fits and n_row & (n_row - 1) == 0 and n_col & (n_col - 1) == 0
    fits = fits and 16 * d * s * chi + 4 * d * s * chi <= 42 * 2**20
    return with_kernels(*args) if fits else without_kernels(*args)


def solution(mesh):
    in_specs = (
        P("row", None, None),
        P(),
        P("row", None, None),
        P("col", None, "row"),
        P("col", None, "row"),
    )
    out_specs = (P("row", "col", None), P(), P("row", "col", None), P("col", "row", None))
    return jax.shard_map(
        on_device, mesh=mesh, in_specs=in_specs, out_specs=out_specs, check_vma=False
    )
```

```python
import functools

import jax
import jax.numpy as jnp
from jax import lax
from jax.experimental import pallas as pl
from jax.experimental.pallas import tpu as pltpu
from jax.sharding import PartitionSpec as P

F32 = jnp.float32
BF16 = jnp.bfloat16
HIGH = lax.Precision.HIGH
NN = (((1,), (0,)), ((), ()))
NT = (((1,), (1,)), ((), ()))
TN = (((0,), (0,)), ((), ()))
BLOCK = 256
TILE = 512


def halves(x):
    hi = x.astype(BF16)
    return hi, (x - hi.astype(F32)).astype(BF16)


def split(x):
    hi = lax.reduce_precision(x, 8, 7)
    return hi.astype(BF16), (x - hi).astype(BF16)


def dot3(xh, xl, yh, yl, dims):
    def dot(x, y):
        return lax.dot_general(x, y, dims, preferred_element_type=F32)

    return dot(xh, yh) + dot(xh, yl) + dot(xl, yh)


def project(xh, xl, wh_ref, wl_ref, oh_ref, ol_ref):
    n = wh_ref.shape[0]
    tile = min(TILE, n)

    def step(i, carry):
        cols = pl.ds(pl.multiple_of(i * tile, tile), tile)
        hi, lo = halves(dot3(xh, xl, wh_ref[cols, :], wl_ref[cols, :], NT))
        oh_ref[:, cols] = hi
        ol_ref[:, cols] = lo
        return carry

    lax.fori_loop(0, n // tile, step, 0)


def gather_pair(ref, start, d, s):
    parts = []
    for k in range(2):
        rows = ref[pl.ds(pl.multiple_of(start + k * d, d), d), :]
        parts.append(jnp.concatenate([rows[:, j * s : (j + 1) * s] for j in range(d)], axis=0))
    return jnp.concatenate(parts, axis=1)


def spread_pair(ref, value, start, d, s):
    for k in range(2):
        rows = [value[j * d : (j + 1) * d, k * s : (k + 1) * s] for j in range(d)]
        ref[pl.ds(pl.multiple_of(start + k * d, d), d), :] = jnp.concatenate(rows, axis=1)


def combine(xh_ref, xl_ref, wh_ref, wl_ref, o_ref):
    n = wh_ref.shape[1]
    tile = min(TILE // 2, n)

    def step(i, carry):
        cols = pl.ds(pl.multiple_of(i * tile, tile), tile)
        o_ref[:, cols] = dot3(xh_ref[...], xl_ref[...], wh_ref[:, cols], wl_ref[:, cols], NN)
        return carry

    lax.fori_loop(0, n // tile, step, 0)


def forward_kernel(d, s, e_ref, sh_ref, sl_ref, rh_ref, rl_ref, ch_ref, cl_ref, left_ref, fh_ref, fl_ref, gh, gl):
    eh, el = halves(e_ref[...])
    project(eh, el, rh_ref, rl_ref, fh_ref, fl_ref)

    def step(i, carry):
        start = i * 2 * d
        x = gather_pair(fh_ref, start, d, s), gather_pair(fl_ref, start, d, s)
        hi, lo = halves(dot3(sh_ref[...], sl_ref[...], *x, NN))
        spread_pair(gh, hi, start, d, s)
        spread_pair(gl, lo, start, d, s)
        return carry

    lax.fori_loop(0, e_ref.shape[0] // (2 * d), step, 0)
    combine(gh, gl, ch_ref, cl_ref, left_ref)


def backward_kernel(
    d, s, e_ref, l_ref, fh_ref, fl_ref, sh_ref, sl_ref, rh_ref, rl_ref, ch_ref, cl_ref,
    edge_ref, right_ref, site_ref, bh, bl, gh, gl,
):
    @pl.when(pl.program_id(0) == 0)
    def _():
        right_ref[...] = jnp.zeros_like(right_ref)
        site_ref[...] = jnp.zeros_like(site_ref)

    lh, ll = halves(l_ref[...])
    project(lh, ll, ch_ref, cl_ref, bh, bl)

    def step(i, carry):
        start = i * 2 * d
        x = gather_pair(bh, start, d, s), gather_pair(bl, start, d, s)
        y = gather_pair(fh_ref, start, d, s), gather_pair(fl_ref, start, d, s)
        hi, lo = halves(dot3(sh_ref[...], sl_ref[...], *x, NN))
        spread_pair(gh, hi, start, d, s)
        spread_pair(gl, lo, start, d, s)
        site_ref[...] += dot3(*x, *y, NT)
        return carry

    lax.fori_loop(0, e_ref.shape[0] // (2 * d), step, 0)
    combine(gh, gl, rh_ref, rl_ref, edge_ref)
    eh, el = halves(e_ref[...])
    tile = min(BLOCK, gh.shape[1])

    def add(i, carry):
        cols = pl.ds(pl.multiple_of(i * tile, tile), tile)
        right_ref[cols, :] += dot3(gh[:, cols], gl[:, cols], eh, el, TN)
        return carry

    lax.fori_loop(0, gh.shape[1] // tile, add, 0)


def whole(shape):
    return pl.BlockSpec(shape, lambda i: (0, 0), pipeline_mode=pl.Buffered(1))


def rows_of(width):
    return pl.BlockSpec((BLOCK, width), lambda i: (i, 0))


PARAMS = pltpu.CompilerParams(dimension_semantics=("arbitrary",), vmem_limit_bytes=58 * 2**20)


def forward(edge, site, right, cot, d, s):
    rows, chi = edge.shape
    wide = d * s
    return pl.pallas_call(
        functools.partial(forward_kernel, d, s),
        grid=(rows // BLOCK,),
        out_shape=[
            jax.ShapeDtypeStruct((rows, chi), F32),
            jax.ShapeDtypeStruct((rows, wide), BF16),
            jax.ShapeDtypeStruct((rows, wide), BF16),
        ],
        in_specs=[rows_of(chi)] + [whole((d * d, d * d))] * 2 + [whole((wide, chi))] * 4,
        out_specs=[rows_of(chi), rows_of(wide), rows_of(wide)],
        scratch_shapes=[pltpu.VMEM((BLOCK, wide), BF16)] * 2,
        compiler_params=PARAMS,
        cost_estimate=pl.CostEstimate(
            flops=12 * rows * wide * chi, bytes_accessed=8 * (rows + wide) * chi, transcendentals=0
        ),
        name="forward",
    )(edge, *site, *right, *cot)


def backward(edge, left, first, site, right, cot, d, s):
    rows, chi = edge.shape
    wide = d * s
    return pl.pallas_call(
        functools.partial(backward_kernel, d, s),
        grid=(rows // BLOCK,),
        out_shape=[
            jax.ShapeDtypeStruct((rows, chi), F32),
            jax.ShapeDtypeStruct((wide, chi), F32),
            jax.ShapeDtypeStruct((d * d, d * d), F32),
        ],
        in_specs=[rows_of(chi)] * 2 + [rows_of(wide)] * 2 + [whole((d * d, d * d))] * 2 + [whole((wide, chi))] * 4,
        out_specs=[rows_of(chi), whole((wide, chi)), whole((d * d, d * d))],
        scratch_shapes=[pltpu.VMEM((BLOCK, wide), BF16)] * 4,
        compiler_params=PARAMS,
        cost_estimate=pl.CostEstimate(
            flops=20 * rows * wide * chi, bytes_accessed=8 * (rows + wide) * chi, transcendentals=0
        ),
        name="backward",
    )(edge, left, *first, *site, *right, *cot)


def swap(x, axis, bit):
    n = lax.axis_size(axis)
    return lax.ppermute(x, axis, [(i, i ^ bit) for i in range(n)])


def gather_row(x):
    s, f, k = x.shape
    whole_bond = lax.all_gather(jnp.transpose(x, (1, 0, 2)), "row", axis=2, tiled=True)
    return whole_bond.reshape(f * s, -1)


def sum_to_row(x, high_first):
    n = lax.axis_size("row")
    me = lax.axis_index("row")
    count = n.bit_length() - 1
    left = list(range(count))[::-1]
    order = [0] + (left[:-1] if high_first else left[:-1][::-1])
    x = x.reshape((2,) * count + (x.shape[0] // n,) + x.shape[1:])
    for b in order:
        axis = left.index(b)
        left.remove(b)
        mine = lax.rem(me // 2**b, 2)
        keep = lax.dynamic_index_in_dim(x, mine, axis, keepdims=False)
        send = lax.dynamic_index_in_dim(x, 1 - mine, axis, keepdims=False)
        x = keep + swap(send, "row", 2**b)
    return x


def sum_all(x):
    for axis in ("row", "col"):
        bit = 1
        while bit < lax.axis_size(axis):
            x = x + swap(x, axis, bit)
            bit *= 2
    return x


def with_kernels(edge_tensor, site_tensor, left_isometry, right_isometry, cotangent, n_front=4, n_back=2):
    a, d, chi = edge_tensor.shape
    s = right_isometry.shape[0]
    right = split(gather_row(right_isometry))
    cot = split(gather_row(cotangent))
    site_front = split(jnp.transpose(site_tensor, (3, 0, 2, 1)).reshape(d * d, d * d))
    site_back = split(jnp.transpose(site_tensor, (2, 1, 3, 0)).reshape(d * d, d * d))
    edge = edge_tensor.reshape(a * d, chi)
    left = left_isometry.reshape(a * d, chi)

    def scatter(terms):
        return lax.psum_scatter(terms.reshape(-1, d, chi), "col", scatter_dimension=1, tiled=True)

    n_front = min(n_front, a * d // BLOCK)
    n_back = min(n_back, n_front)
    lefts, firsts = [], []
    for x in jnp.split(edge, n_front):
        terms, fh, fl = forward(x, site_front, right, cot, d, s)
        lefts.append(scatter(terms))
        firsts.append((fh, fl))
    join = n_front // n_back
    edges, rights, sites = [], [], []
    for i, (x, y) in enumerate(zip(jnp.split(edge, n_back), jnp.split(left, n_back))):
        part = firsts[i * join : (i + 1) * join]
        first = tuple(jnp.concatenate([p[k] for p in part], 0) for k in range(2))
        edge_terms, right_terms, site_terms = backward(x, y, first, site_back, right, cot, d, s)
        edges.append(scatter(edge_terms))
        rights.append(right_terms)
        sites.append(site_terms)
    total = sum(rights)
    half = chi // 2
    right_sum = jnp.concatenate([sum_to_row(total[:, :half], True), sum_to_row(total[:, half:], False)], 1)
    right_gradient = jnp.transpose(right_sum.reshape(-1, s, chi), (1, 0, 2))
    site_gradient = jnp.transpose(sum_all(sum(sites)).reshape(d, d, d, d), (1, 3, 2, 0))
    return jnp.concatenate(edges, 0), site_gradient, jnp.concatenate(lefts, 0), right_gradient


def ein(spec, x, y):
    return jnp.einsum(spec, x, y, precision=HIGH)


def without_kernels(edge_tensor, site_tensor, left_isometry, right_isometry, cotangent):
    edge = jnp.transpose(edge_tensor, (1, 0, 2))
    left = jnp.transpose(left_isometry, (1, 0, 2))
    right = lax.all_gather(jnp.transpose(right_isometry, (1, 0, 2)), "row", axis=2, tiled=True)
    cot = lax.all_gather(jnp.transpose(cotangent, (1, 0, 2)), "row", axis=2, tiled=True)
    first = ein("eab,fsb->efas", edge, right)
    second = ein("defg,efas->dgas", site_tensor, first)
    left_terms = ein("dgas,gsc->dac", second, cot)
    left_gradient = lax.psum_scatter(left_terms, "col", scatter_dimension=0, tiled=True)
    back_second = ein("dac,gsc->dgas", left, cot)
    back_first = ein("defg,dgas->efas", site_tensor, back_second)
    edge_terms = ein("efas,fsb->eab", back_first, right)
    edge_gradient = lax.psum_scatter(edge_terms, "col", scatter_dimension=0, tiled=True)
    right_terms = ein("efas,eab->sfb", back_first, edge)
    right_gradient = lax.psum_scatter(right_terms, "row", scatter_dimension=1, tiled=True)
    site_terms = ein("efas,dgas->efdg", first, back_second)
    site_gradient = jnp.transpose(lax.psum(site_terms, ("row", "col")), (2, 0, 1, 3))
    return (
        jnp.transpose(edge_gradient, (1, 0, 2)),
        site_gradient,
        jnp.transpose(left_gradient, (1, 0, 2)),
        right_gradient,
    )


def on_device(*args):
    a, d, chi = args[0].shape
    s = args[3].shape[0]
    n_row, n_col = lax.axis_size("row"), lax.axis_size("col")
    fits = s % 128 == 0 and chi % 256 == 0 and (a * d) % BLOCK == 0 and d % 16 == 0 and n_row > 1
    fits = fits and n_row & (n_row - 1) == 0 and n_col & (n_col - 1) == 0
    fits = fits and 16 * d * s * chi + 4 * d * s * chi <= 42 * 2**20
    return with_kernels(*args) if fits else without_kernels(*args)


def solution(mesh):
    in_specs = (
        P("row", None, None),
        P(),
        P("row", None, None),
        P("col", None, "row"),
        P("col", None, "row"),
    )
    out_specs = (P("row", "col", None), P(), P("row", "col", None), P("col", "row", None))
    return jax.shard_map(
        on_device, mesh=mesh, in_specs=in_specs, out_specs=out_specs, check_vma=False
    )
```
